32 devices in a mesh: expert: 8 (over z, x), dp: 4 (over y, core).
Axes of the slice: x: 2, y: 2, z: 4, core: 2. Of those that a mesh axis runs over, the one named last changes fastest.
Arguments:
- tokens: bfloat16 [4096, 2048], P(('expert', 'dp')), may hold values from -6 to 6
- d_out: bfloat16 [4096, 2048], P(('expert', 'dp')), may hold values from -6 to 6
- router_logits: float32 [4096, 16], P(('expert', 'dp')), may hold values from -15 to 420
- routes: int32 [4096, 1], P(('expert', 'dp')), may hold values from 0 to 15; in each aligned block of 128 rows (0 to 127, 128 to 255, ...) at most 16 rows name the same one
- gate_weight: bfloat16 [16, 1408, 2048], P('expert', 'dp'), may hold values from -0.125 to 0.125
- up_weight: bfloat16 [16, 1408, 2048], P('expert', 'dp'), may hold values from -0.125 to 0.125
- down_weight: bfloat16 [16, 1408, 2048], P('expert', 'dp'), may hold values from -0.15625 to 0.15625
Outputs:
- d_tokens: bfloat16 [4096, 2048], P(('expert', 'dp'))
- d_logits: float32 [4096, 16], P(('expert', 'dp'))
- d_gate_weight: bfloat16 [16, 1408, 2048], P('expert', 'dp')
- d_up_weight: bfloat16 [16, 1408, 2048], P('expert', 'dp')
- d_down_weight: bfloat16 [16, 1408, 2048], P('expert', 'dp')
The draws below stay inside these ranges and needn't reach their ends.
Inputs may be any that keep to these rules, and one draw needn't show every extreme that they name: `routes`: in each aligned block of 128 rows (the rows of one device) no expert is named by more than 16 rows, a bound that some block reaches.
All inputs are finite; a program needn't handle non-finite values.
Results may differ from the reference program's by a relative error of at most 0.011.
Values may be sent and summed in bfloat16 or wider, within the bound.
A program may use at most 128 MiB of HBM per device.

```python
import math
import jax
import jax.numpy as jnp
import numpy as np
from jax import lax

D = 2048
FF = 1408
TOK_DEV = 128
ITERS = 8
EXPERTS = 16
FF_DEV = 352
CAP = 16
TOKENS = 4096


def shared_direction(key):
    return jnp.clip(jax.random.normal(key, (1, D), jnp.float32), -4.0, 4.0)


def draw_tokens(key, part):
    direction = shared_direction(key)
    key = jax.random.fold_in(key, 23)
    noise = jnp.clip(jax.random.normal(key, (TOKENS, D), jnp.float32), -4.0, 4.0)
    return jnp.clip(0.7 * noise + 0.7 * direction, -6.0, 6.0).astype(jnp.bfloat16)


def draw_d_out(key, part):
    direction = shared_direction(key)
    key = jax.random.fold_in(key, 29)
    noise = jnp.clip(jax.random.normal(key, (TOKENS, D), jnp.float32), -4.0, 4.0)
    return jnp.clip(0.7 * noise + 0.7 * direction, -6.0, 6.0).astype(jnp.bfloat16)


def draw_router_logits(key, part):
    key = jax.random.fold_in(key, 17)
    subkeys = jax.random.split(key, 14)
    position = jnp.arange(TOKENS, dtype=jnp.float32) * (2.0 / TOKENS) - 1.0
    column_tilt = jax.random.uniform(subkeys[0], (1, EXPERTS), jnp.float32, -0.6, 0.6)
    expert_group = jax.random.permutation(subkeys[1], EXPERTS) % 4
    group_shares = jnp.log(jnp.array([0.46, 0.28, 0.16, 0.1], jnp.float32))
    token_group = jax.random.categorical(subkeys[2], group_shares, shape=(TOKENS,))
    strength = jax.random.uniform(subkeys[3], (TOKENS, 1), jnp.float32, 2.0, 9.0)
    affinity = strength * (token_group[:, None] == expert_group[None, :]).astype(jnp.float32)
    silent = jax.random.randint(subkeys[4], (), 0, EXPERTS)
    column = jnp.arange(EXPERTS)[None, :]
    base_logits = 110.0 + affinity + jnp.clip(1.5 * jax.random.normal(subkeys[6], (TOKENS, EXPERTS), jnp.float32), -6.0, 6.0)
    base_logits = base_logits + column_tilt * position[:, None]
    quiet_column = -15.0 + jax.random.uniform(subkeys[13], (TOKENS, 1), jnp.float32, 0.0, 2.0)
    return jnp.where(column == silent, quiet_column, base_logits)


def block_scale(own_key, shape, pieces, low, largest):
    level, own = 1.0, jax.random.fold_in(own_key, 6)
    for dim, shards_of in pieces:
        draws = jnp.exp(jax.random.uniform(jax.random.fold_in(own, dim), (shards_of,), jnp.float32, low / len(pieces), largest / len(pieces)))
        level = level * jnp.repeat(draws, shape[dim] // shards_of).reshape([-1 if axis == dim else 1 for axis in range(len(shape))])
    return level


def deal_out(stream_key, own, number, rows, amount, top, bound, lean):
    ranking = jax.random.permutation(stream_key, amount)
    packed, usual = portions_of(amount, rows * top, bound, lean, True), portions_of(amount, rows * top, bound, lean, False)
    places = jnp.arange(amount)

    def named(sizes, rotation):
        used = int((sizes > 0).sum())
        fixed = max(1, used // 4)
        moved = fixed + (places - fixed + rotation * (used - fixed)) % max(1, amount - fixed)
        return jnp.zeros((amount,), jnp.int32).at[ranking[jnp.where(places < fixed, places, moved)]].set(jnp.asarray(sizes, jnp.int32))

    sizes = jnp.where(number % 4 == 0, named(packed, number // 4), named(usual, number - number // 4 - 1))
    mixed = jax.random.permutation(jax.random.fold_in(own, 3), amount)
    donor, receiver = mixed[0:amount // 2 * 2:2], mixed[1:amount // 2 * 2:2]
    slack = jnp.minimum(sizes[donor] - 1, bound - sizes[receiver]) // 2
    slack = jnp.where((donor == ranking[0]) | (receiver == ranking[0]) | (sizes[receiver] == 0), 0, jnp.maximum(slack, 0))
    moved = jax.random.randint(jax.random.fold_in(own, 4), (amount // 2,), 0, 1 << 20) % (slack + 1)
    sizes = sizes.at[donor].add(-moved).at[receiver].add(moved)
    items = jnp.searchsorted(jnp.cumsum(sizes), jnp.arange(rows * top), side="right").astype(jnp.int32)
    table = items.reshape(top, rows).T
    table = table[jax.random.permutation(jax.random.fold_in(own, 1), rows)]
    rotation = jax.random.randint(jax.random.fold_in(own, 2), (rows, 1), 0, top)
    return jnp.take_along_axis(table, (jnp.arange(top)[None, :] + rotation) % top, axis=1)


def portions_of(count, total, reach, slope, full):
    portions = [(1 << 20) // math.isqrt(standing ** slope) + 1 for standing in range(1, count + 1)]
    largest = reach if full else min(reach, max(-(-total // count), total * portions[0] // sum(portions)))
    least = 1 if total - largest >= count - 1 else 0
    given, rest = [largest] + [least] * (count - 1), total - largest - least * (count - 1)
    while rest > 0:
        free = [i for i in range(1, count) if given[i] < largest] or [i for i in range(1, count) if given[i] < reach]
        whole, remaining = sum([portions[i] for i in free]), rest
        for i in free:
            extra = min(reach - given[i], max(1, remaining * portions[i] // whole), rest)
            given[i] = given[i] + extra
            rest = rest - extra
    return np.array(given)


def centred(rng, dims, scale, reach, pieces=(), held_as=jnp.bfloat16):
    entries = scale * jax.random.normal(rng, dims, jnp.float32)
    if pieces:
        entries = entries * block_scale(rng, dims, pieces, -0.22, 0.18)
    return jnp.clip(entries, -reach, reach).astype(held_as)


def setup_inputs(seed: int = 0) -> dict:
    keys = jax.random.split(jax.random.key(seed), 8)
    tokens = draw_tokens(jax.random.fold_in(keys[7], 71), 0)
    d_out = draw_d_out(jax.random.fold_in(keys[7], 71), 0)
    router_logits = draw_router_logits(jax.random.fold_in(keys[7], 71), 0)
    routes_keys = jax.random.split(jax.random.fold_in(keys[3], 1), TOKENS // TOK_DEV)
    routes_turns = jax.random.permutation(jax.random.fold_in(keys[3], 3), TOKENS // TOK_DEV)
    routes = jax.vmap(lambda own, number: deal_out(jax.random.fold_in(keys[3], 2), own, number, TOK_DEV, EXPERTS, 1, CAP, 0))(routes_keys, routes_turns).reshape((TOKENS, 1))
    gate_weight = centred(keys[4], (EXPERTS, FF, D), D ** -0.5, 0.125, ((0, 8), (1, 4)))
    up_weight = centred(keys[5], (EXPERTS, FF, D), D ** -0.5, 0.125, ((0, 8), (1, 4)))
    down_weight = centred(keys[6], (EXPERTS, FF, D), FF ** -0.5, 0.15625, ((0, 8), (1, 4)))
    return {"tokens": tokens, "d_out": d_out, "router_logits": router_logits, "routes": routes, "gate_weight": gate_weight, "up_weight": up_weight, "down_weight": down_weight}


def potentials(logits):
    offset = jnp.log(jnp.asarray(TOKENS / EXPERTS, logits.dtype))
    col_now = jnp.zeros((EXPERTS,), logits.dtype)
    for sweep_k in range(ITERS):
        row_now = -jax.nn.logsumexp(logits + col_now[None, :], axis=1)
        col_now = offset - jax.nn.logsumexp(logits + row_now[:, None], axis=0)
    return col_now

def gates_of(logits, chosen):
    col_now = potentials(logits)
    soft_probs = jax.nn.softmax(logits + col_now[None, :], axis=1)
    return EXPERTS * lax.optimization_barrier(jnp.sum(soft_probs * chosen, axis=1))

def expert_backward(rows_x, rows_dy, rows_gating, w_gate, w_up, w_down):
    pre_gate = jnp.dot(rows_x, w_gate.T, preferred_element_type=jnp.float32)
    pre_up = jnp.dot(rows_x, w_up.T, preferred_element_type=jnp.float32)
    backward = jnp.dot(rows_dy, w_down.T, preferred_element_type=jnp.float32)
    sigmoid = jax.nn.sigmoid(pre_gate)
    activated = pre_gate * sigmoid
    hidden = (activated * pre_up).astype(jnp.bfloat16)
    hidden_wide = hidden.astype(jnp.float32)
    gate_column = rows_gating.astype(jnp.float32)[:, None]
    scaled_back = backward * gate_column
    d_pre_gate = (scaled_back * pre_up * sigmoid * (1.0 + pre_gate * (1.0 - sigmoid))).astype(jnp.bfloat16)
    d_pre_up = (scaled_back * activated).astype(jnp.bfloat16)
    d_rows = jnp.zeros((rows_x.shape[0], rows_x.shape[1]), jnp.float32)
    gating_total = jnp.zeros((rows_x.shape[0],), jnp.float32)
    for block_index in range(FF // FF_DEV):
        lower_edge = block_index * FF_DEV
        upper_edge = lower_edge + FF_DEV
        block_rows = jnp.dot(d_pre_gate[:, lower_edge:upper_edge], w_gate[lower_edge:upper_edge], preferred_element_type=jnp.float32) + jnp.dot(d_pre_up[:, lower_edge:upper_edge], w_up[lower_edge:upper_edge], preferred_element_type=jnp.float32)
        d_rows = d_rows + lax.optimization_barrier(block_rows.astype(jnp.bfloat16)).astype(jnp.float32)
        block_gating = lax.optimization_barrier(jnp.sum(hidden_wide[:, lower_edge:upper_edge] * backward[:, lower_edge:upper_edge], axis=1))
        gating_total = gating_total + lax.optimization_barrier(block_gating.astype(jnp.bfloat16)).astype(jnp.float32)
    gating_part = lax.optimization_barrier(gating_total.astype(jnp.bfloat16))
    scaled_out = (gate_column * rows_dy.astype(jnp.float32)).astype(jnp.bfloat16)
    d_down = jnp.dot(hidden.T, scaled_out, preferred_element_type=jnp.float32).astype(jnp.bfloat16)
    d_gate_w = jnp.dot(d_pre_gate.T, rows_x, preferred_element_type=jnp.float32).astype(jnp.bfloat16)
    d_up_w = jnp.dot(d_pre_up.T, rows_x, preferred_element_type=jnp.float32).astype(jnp.bfloat16)
    return (d_rows.astype(jnp.bfloat16), gating_part, d_gate_w, d_up_w, d_down)

def reference(tokens, d_out, router_logits, routes, gate_weight, up_weight, down_weight):
    route_ids = routes[:, 0].astype(jnp.int32)
    labels = jnp.arange(EXPERTS, dtype=jnp.int32)
    hit_table = (route_ids[:, None] == labels[None, :]).astype(jnp.int32)
    slot_rank = lax.optimization_barrier(jnp.sum((jnp.cumsum(hit_table, axis=0) - hit_table) * hit_table, axis=1)).astype(jnp.int32)
    bound_rows = 2 * TOKENS // EXPERTS
    slot_index = (route_ids * bound_rows + slot_rank).astype(jnp.int32)
    slot_table = jnp.full((EXPERTS * bound_rows,), TOKENS, jnp.int32).at[slot_index].set(jnp.arange(TOKENS, dtype=jnp.int32))
    chosen = hit_table.astype(router_logits.dtype)
    gating = gates_of(router_logits, chosen)
    gating_low = lax.optimization_barrier(gating.astype(jnp.bfloat16))
    zero_row = jnp.zeros((1, tokens.shape[1]), tokens.dtype)
    padded_x = jnp.concatenate([tokens, zero_row], axis=0)
    padded_dy = jnp.concatenate([d_out, zero_row], axis=0)
    padded_gating = jnp.concatenate([gating_low, jnp.zeros((1,), gating_low.dtype)])

    def one_expert(expert_items):
        row_index, w_gate, w_up, w_down = expert_items
        return expert_backward(padded_x[row_index], padded_dy[row_index], padded_gating[row_index], w_gate, w_up, w_down)
    d_rows, gating_rows, d_gate_weight, d_up_weight, d_down_weight = lax.map(one_expert, (slot_table.reshape(EXPERTS, bound_rows), gate_weight, up_weight, down_weight))
    d_tokens = d_rows.reshape(EXPERTS * bound_rows, -1)[slot_index]
    d_gating = gating_rows.reshape(-1)[slot_index]
    unused, pullback = jax.vjp(lambda logits: gates_of(logits, chosen), router_logits)
    d_logits = pullback(d_gating.astype(router_logits.dtype))[0]
    return (d_tokens, d_logits, d_gate_weight, d_up_weight, d_down_weight)
```

```python
import functools
import math

import jax
import jax.numpy as jnp
from jax import lax
from jax.experimental import pallas as pl
from jax.experimental.pallas import tpu as pltpu
from jax.sharding import PartitionSpec as P

ITERS = 8
LANES = 128
CHUNK = 8
MESH = pl.DeviceIdType.MESH
VMEM_LIMIT = 48 * 1024 * 1024


def place(n_expert, n_data):
    my_e, my_d = lax.axis_index("expert"), lax.axis_index("dp")
    half, core = my_d // 2, my_d % 2
    sibling = half * 2 + (1 - core)
    across = (1 - half) * 2 + core
    diagonal = (1 - half) * 2 + (1 - core)
    return my_e, my_d, half, core, sibling, across, diagonal


def sinkhorn_step(k, offset, experts, sources, small_out, rows_out, cols_out):
    col = cols_out[k]

    def row_pass(step, top):
        at = pl.ds(step * CHUNK, CHUNK)
        logits = small_out[at, :experts, :]
        shifted = logits + col[None]
        high = jnp.max(shifted, axis=1, keepdims=True)
        row = -(high + jnp.log(jnp.sum(jnp.exp(shifted - high), axis=1, keepdims=True)))
        rows_out[k, at, :, :] = row
        return jnp.maximum(top, jnp.max(logits + row, axis=0))

    top = lax.fori_loop(
        0, sources // CHUNK, row_pass, jnp.full((experts, LANES), -1e30, jnp.float32)
    )
    top = jnp.max(top, axis=1, keepdims=True)

    def col_pass(step, total):
        at = pl.ds(step * CHUNK, CHUNK)
        logits = small_out[at, :experts, :]
        return total + jnp.sum(jnp.exp(logits + rows_out[k, at, :, :] - top[None]), axis=0)

    total = lax.fori_loop(
        0, sources // CHUNK, col_pass, jnp.zeros((experts, LANES), jnp.float32)
    )
    total = jnp.sum(total, axis=1, keepdims=True)
    cols_out[k + 1] = jnp.broadcast_to(offset - (top + jnp.log(total)), (experts, LANES))


def dispatch_kernel(
    n_expert, n_data, offset,
    send_ref, small_ref, got_ref, small_out, rows_out, cols_out,
    big_send, big_recv, small_send, small_recv, local_sem,
):
    my_e, my_d, half, core, sibling, across, diagonal = place(n_expert, n_data)
    me = my_e * n_data + my_d
    sources = n_expert * n_data
    experts = cols_out.shape[1]

    barrier = pltpu.get_barrier_semaphore()

    def greet(i, carry):
        pl.semaphore_signal(
            barrier, inc=1, device_id=(lax.rem(my_e + i, n_expert), my_d), device_id_type=MESH
        )
        return carry

    lax.fori_loop(1, n_expert, greet, 0)
    pl.semaphore_signal(barrier, inc=1, device_id=(my_e, sibling), device_id_type=MESH)
    pl.semaphore_signal(barrier, inc=1, device_id=(my_e, across), device_id_type=MESH)
    pl.semaphore_wait(barrier, n_expert + 1)

    def small_copy(src, source, leg, i, device):
        return pltpu.make_async_remote_copy(
            src_ref=src, dst_ref=small_out.at[source],
            send_sem=small_send.at[leg, i], recv_sem=small_recv.at[source],
            device_id=device, device_id_type=MESH,
        )

    def big_copy(src, source, leg, i, device):
        return pltpu.make_async_remote_copy(
            src_ref=src, dst_ref=got_ref.at[:, :, source],
            send_sem=big_send.at[leg, i], recv_sem=big_recv.at[source],
            device_id=device, device_id_type=MESH,
        )

    def first_small(i, carry):
        other = lax.rem(my_e + i, n_expert)
        small_copy(small_ref.at[other], me, 0, i, (other, my_d)).start()
        return carry

    def first_big(i, carry):
        other = lax.rem(my_e + i, n_expert)
        big_copy(send_ref.at[other], me, 0, i, (other, my_d)).start()
        return carry

    lax.fori_loop(1, n_expert, first_small, 0)
    lax.fori_loop(1, n_expert, first_big, 0)
    own = pltpu.make_async_copy(send_ref.at[my_e], got_ref.at[:, :, me], local_sem)
    own.start()
    small_out[me] = small_ref[my_e]
    cols_out[0] = jnp.zeros((experts, LANES), jnp.float32)

    def origin(i, lane):
        return lax.rem(my_e + n_expert - i, n_expert) * n_data + lane

    def forward_small(i, carry):
        source = origin(i, my_d)

        @pl.when(i > 0)
        def _():
            small_copy(small_out.at[source], source, 0, i, (my_e, my_d)).wait_recv()

        small_copy(small_out.at[source], source, 1, i, (my_e, across)).start()
        small_copy(small_out.at[source], source, 2, i, (my_e, sibling)).start()
        return carry

    lax.fori_loop(0, n_expert, forward_small, 0)

    own.wait()
    big_copy(got_ref.at[:, :, me], me, 1, 0, (my_e, across)).start()
    big_copy(got_ref.at[:, :, me], me, 2, 0, (my_e, sibling)).start()

    def cross_small(i, carry):
        source = origin(i, across)
        small_copy(small_out.at[source], source, 1, i, (my_e, across)).wait_recv()
        small_copy(small_out.at[source], source, 3, i, (my_e, sibling)).start()
        return carry

    lax.fori_loop(0, n_expert, cross_small, 0)

    def last_small(i, carry):
        for lane in (sibling, diagonal):
            source = origin(i, lane)
            small_copy(small_out.at[source], source, 2, i, (my_e, sibling)).wait_recv()
        return carry

    lax.fori_loop(0, n_expert, last_small, 0)

    def forward_big(i):
        source = origin(i, my_d)
        block = got_ref.at[:, :, source]
        big_copy(block, source, 0, i, (my_e, my_d)).wait_recv()
        big_copy(block, source, 1, i, (my_e, across)).start()
        big_copy(block, source, 2, i, (my_e, sibling)).start()

    def step(i, carry):
        sinkhorn_step(i, offset, experts, sources, small_out, rows_out, cols_out)

        @pl.when(i + 1 < n_expert)
        def _():
            forward_big(i + 1)

        return carry

    lax.fori_loop(0, ITERS, step, 0)

    def plain_step(i, carry):
        forward_big(i)
        return carry

    if n_expert > ITERS + 1:
        lax.fori_loop(ITERS + 1, n_expert, plain_step, 0)

    def cross_big(i, carry):
        source = origin(i, across)
        block = got_ref.at[:, :, source]
        big_copy(block, source, 1, i, (my_e, across)).wait_recv()
        big_copy(block, source, 3, i, (my_e, sibling)).start()
        return carry

    lax.fori_loop(0, n_expert, cross_big, 0)

    def last_big(i, carry):
        for lane in (sibling, diagonal):
            source = origin(i, lane)
            big_copy(got_ref.at[:, :, source], source, 2, i, (my_e, sibling)).wait_recv()
        return carry

    lax.fori_loop(0, n_expert, last_big, 0)

    def drain(i, carry):
        block = got_ref.at[:, :, me]
        for leg in (1, 2, 3):
            small_copy(small_out.at[me], me, leg, i, (my_e, sibling)).wait_send()
            big_copy(block, me, leg, i, (my_e, sibling)).wait_send()

        @pl.when(i > 0)
        def _():
            small_copy(small_out.at[me], me, 0, i, (my_e, sibling)).wait_send()
            big_copy(block, me, 0, i, (my_e, sibling)).wait_send()

        return carry

    lax.fori_loop(0, n_expert, drain, 0)


def dispatch(send, small, n_expert, n_data, offset):
    sources = n_expert * n_data
    experts = small.shape[1] // 2
    _, kinds, split, rows, width = send.shape
    return pl.pallas_call(
        functools.partial(dispatch_kernel, n_expert, n_data, offset),
        out_shape=(
            jax.ShapeDtypeStruct((kinds, split, sources, rows, width), jnp.bfloat16),
            jax.ShapeDtypeStruct((sources, 2 * experts, LANES), jnp.float32),
            jax.ShapeDtypeStruct((ITERS, sources, 1, LANES), jnp.float32),
            jax.ShapeDtypeStruct((ITERS + 1, experts, LANES), jnp.float32),
        ),
        in_specs=[pl.BlockSpec(memory_space=pl.ANY), pl.BlockSpec(memory_space=pltpu.VMEM)],
        out_specs=(
            pl.BlockSpec(memory_space=pl.ANY),
            pl.BlockSpec(memory_space=pltpu.VMEM),
            pl.BlockSpec(memory_space=pltpu.VMEM),
            pl.BlockSpec(memory_space=pltpu.VMEM),
        ),
        scratch_shapes=[
            pltpu.SemaphoreType.DMA((4, n_expert)),
            pltpu.SemaphoreType.DMA((sources,)),
            pltpu.SemaphoreType.DMA((4, n_expert)),
            pltpu.SemaphoreType.DMA((sources,)),
            pltpu.SemaphoreType.DMA,
        ],
        compiler_params=pltpu.CompilerParams(
            collective_id=0, has_side_effects=True, vmem_limit_bytes=VMEM_LIMIT
        ),
        name="dispatch",
    )(send, small)


def add_blocks(left, right):
    return (left.astype(jnp.float32) + right.astype(jnp.float32)).astype(jnp.bfloat16)


def column_chain(offset, experts, sources, tiles, logits_ref, rows_ref, cols_ref, chain_out):
    first = jnp.sum(tiles[:, 1:2, :], axis=0)
    lane = lax.broadcasted_iota(jnp.int32, (experts, LANES), 1)
    sub = lax.broadcasted_iota(jnp.int32, (experts, LANES), 0)
    d_col = jnp.sum(
        jnp.where(lane == sub, jnp.broadcast_to(first, (experts, LANES)), 0.0),
        axis=1,
        keepdims=True,
    )
    chain_out[ITERS - 1] = jnp.broadcast_to(d_col, (experts, LANES))

    def sweep(step, d_now):
        k = ITERS - 1 - step
        col_after, col_before = cols_ref[k + 1], cols_ref[k]

        def part(piece, total):
            at = pl.ds(piece * CHUNK, CHUNK)
            base = logits_ref[at, :experts, :] + rows_ref[k, at, :, :]
            pulled = jnp.sum(
                d_now[None] * jnp.exp(base + (col_after - offset)[None]), axis=1, keepdims=True
            )
            return total + jnp.sum(pulled * jnp.exp(base + col_before[None]), axis=0)

        total = lax.fori_loop(
            0, sources // CHUNK, part, jnp.zeros((experts, LANES), jnp.float32)
        )
        d_next = jnp.broadcast_to(jnp.sum(total, axis=1, keepdims=True), (experts, LANES))
        chain_out[k - 1] = d_next
        return d_next

    lax.fori_loop(0, ITERS - 1, sweep, jnp.broadcast_to(d_col, (experts, LANES)))


def collect_kernel(
    n_expert, n_data, offset,
    d_ref, tile_ref, logits_ref, rows_ref, cols_ref,
    home, tiles, chain_out,
    pair, cross,
    core_send, core_recv, y_send, y_recv, home_send, home_recv, tile_send, tile_recv,
):
    my_e, my_d, half, core, sibling, across, diagonal = place(n_expert, n_data)
    me = my_e * n_data + my_d
    sources = n_expert * n_data
    experts = cols_ref.shape[1]
    other_core, other_half = 1 - core, 1 - half

    barrier = pltpu.get_barrier_semaphore()

    def peer(i):
        index = lax.rem(me + i, sources)
        return index, (index // n_data, lax.rem(index, n_data))

    def greet(i, carry):
        pl.semaphore_signal(barrier, inc=1, device_id=peer(i)[1], device_id_type=MESH)
        return carry

    lax.fori_loop(1, sources, greet, 0)
    pl.semaphore_wait(barrier, sources - 1)

    def tile_copy(i):
        index, device = peer(i)
        return pltpu.make_async_remote_copy(
            src_ref=tile_ref.at[index], dst_ref=tiles.at[me],
            send_sem=tile_send.at[i], recv_sem=tile_recv.at[me],
            device_id=device, device_id_type=MESH,
        )

    def core_copy(e, y):
        return pltpu.make_async_remote_copy(
            src_ref=d_ref.at[:, e * n_data + y * 2 + other_core], dst_ref=pair.at[:, e * 2 + y],
            send_sem=core_send.at[e * 2 + y], recv_sem=core_recv.at[e * 2 + y],
            device_id=(my_e, sibling), device_id_type=MESH,
        )

    def y_copy(e):
        return pltpu.make_async_remote_copy(
            src_ref=pair.at[:, e * 2 + other_half], dst_ref=cross.at[:, e],
            send_sem=y_send.at[e], recv_sem=y_recv.at[e],
            device_id=(my_e, across), device_id_type=MESH,
        )

    def home_copy(e):
        return pltpu.make_async_remote_copy(
            src_ref=cross.at[:, e], dst_ref=home.at[my_e],
            send_sem=home_send.at[e], recv_sem=home_recv.at[my_e],
            device_id=(e, my_d), device_id_type=MESH,
        )

    def order(i):
        return lax.rem(my_e + 1 + i, n_expert)

    def start_core(i, carry):
        e = order(i)
        core_copy(e, other_half).start()
        core_copy(e, half).start()
        return carry

    lax.fori_loop(0, n_expert, start_core, 0)

    def start_tile(i, carry):
        tile_copy(i).start()
        return carry

    lax.fori_loop(1, sources, start_tile, 0)
    tiles[me] = tile_ref[me]

    def fold_core(i, carry):
        e = order(i)
        core_copy(e, other_half).wait_recv()
        away, near = e * 2 + other_half, e * 2 + half
        pair[:, away] = add_blocks(pair[:, away], d_ref[:, e * n_data + other_half * 2 + core])
        y_copy(e).start()
        core_copy(e, half).wait_recv()
        pair[:, near] = add_blocks(pair[:, near], d_ref[:, e * n_data + half * 2 + core])
        return carry

    lax.fori_loop(0, n_expert, fold_core, 0)

    def fold_y(i, carry):
        e = order(i)
        y_copy(e).wait_recv()
        cross[:, e] = add_blocks(cross[:, e], pair[:, e * 2 + half])

        @pl.when(i < n_expert - 1)
        def _():
            home_copy(e).start()

        return carry

    lax.fori_loop(0, n_expert, fold_y, 0)
    home[my_e] = cross[:, my_e]

    def tile_arrival(i, carry):
        index, device = peer(i)
        pltpu.make_async_remote_copy(
            src_ref=tile_ref.at[index], dst_ref=tiles.at[index],
            send_sem=tile_send.at[i], recv_sem=tile_recv.at[index],
            device_id=device, device_id_type=MESH,
        ).wait_recv()
        return carry

    lax.fori_loop(1, sources, tile_arrival, 0)
    column_chain(offset, experts, sources, tiles, logits_ref, rows_ref, cols_ref, chain_out)

    def home_arrival(i, carry):
        e = order(i)
        pltpu.make_async_remote_copy(
            src_ref=cross.at[:, e], dst_ref=home.at[e],
            send_sem=home_send.at[e], recv_sem=home_recv.at[e],
            device_id=(e, my_d), device_id_type=MESH,
        ).wait_recv()
        home_copy(e).wait_send()
        return carry

    lax.fori_loop(0, n_expert - 1, home_arrival, 0)

    def drain(i, carry):
        core_copy(i, 0).wait_send()
        core_copy(i, 1).wait_send()
        y_copy(i).wait_send()
        return carry

    lax.fori_loop(0, n_expert, drain, 0)

    def drain_tiles(i, carry):
        tile_copy(i).wait_send()
        return carry

    lax.fori_loop(1, sources, drain_tiles, 0)


def collect(d_all, tile, logits, rows, cols, n_expert, n_data, offset):
    split, sources, height, width = d_all.shape
    experts = cols.shape[1]
    vmem = pl.BlockSpec(memory_space=pltpu.VMEM)
    return pl.pallas_call(
        functools.partial(collect_kernel, n_expert, n_data, offset),
        out_shape=(
            jax.ShapeDtypeStruct((n_expert, split, height, width), jnp.bfloat16),
            jax.ShapeDtypeStruct(tile.shape, jnp.float32),
            jax.ShapeDtypeStruct((ITERS, experts, LANES), jnp.float32),
        ),
        in_specs=[vmem] * 5,
        out_specs=(vmem, vmem, vmem),
        scratch_shapes=[
            pltpu.VMEM((split, 2 * n_expert, height, width), jnp.bfloat16),
            pltpu.VMEM((split, n_expert, height, width), jnp.bfloat16),
            pltpu.SemaphoreType.DMA((2 * n_expert,)),
            pltpu.SemaphoreType.DMA((2 * n_expert,)),
            pltpu.SemaphoreType.DMA((n_expert,)),
            pltpu.SemaphoreType.DMA((n_expert,)),
            pltpu.SemaphoreType.DMA((n_expert,)),
            pltpu.SemaphoreType.DMA((n_expert,)),
            pltpu.SemaphoreType.DMA((sources,)),
            pltpu.SemaphoreType.DMA((sources,)),
        ],
        compiler_params=pltpu.CompilerParams(
            collective_id=1, has_side_effects=True, vmem_limit_bytes=VMEM_LIMIT
        ),
        name="collect",
    )(d_all, tile, logits, rows, cols)


def expert_backward(rows_x, rows_dy, gate_row, w_gate, w_up, w_down):
    last_pair = (((1,), (1,)), ((), ()))
    first_pair = (((0,), (0,)), ((), ()))
    pre_gate = lax.dot_general(w_gate, rows_x, last_pair, preferred_element_type=jnp.float32)
    pre_up = lax.dot_general(w_up, rows_x, last_pair, preferred_element_type=jnp.float32)
    backward = lax.dot_general(w_down, rows_dy, last_pair, preferred_element_type=jnp.float32)
    sigmoid = jax.nn.sigmoid(pre_gate)
    activated = pre_gate * sigmoid
    hidden = (activated * pre_up).astype(jnp.bfloat16)
    gating_part = jnp.sum(hidden.astype(jnp.float32) * backward, axis=0)
    scaled_back = backward * gate_row[None, :]
    d_pre_gate = (scaled_back * pre_up * sigmoid * (1.0 + pre_gate * (1.0 - sigmoid))).astype(
        jnp.bfloat16
    )
    d_pre_up = (scaled_back * activated).astype(jnp.bfloat16)
    d_rows = lax.dot_general(
        d_pre_gate, w_gate, first_pair, preferred_element_type=jnp.float32
    ) + lax.dot_general(d_pre_up, w_up, first_pair, preferred_element_type=jnp.float32)
    scaled_out = (gate_row[:, None] * rows_dy.astype(jnp.float32)).astype(jnp.bfloat16)
    d_down = jnp.dot(hidden, scaled_out, preferred_element_type=jnp.float32).astype(jnp.bfloat16)
    d_gate_w = jnp.dot(d_pre_gate, rows_x, preferred_element_type=jnp.float32).astype(jnp.bfloat16)
    d_up_w = jnp.dot(d_pre_up, rows_x, preferred_element_type=jnp.float32).astype(jnp.bfloat16)
    return (d_rows.astype(jnp.bfloat16), gating_part, d_gate_w, d_up_w, d_down)


def body(tokens, d_out, router_logits, routes, gate_weight, up_weight, down_weight):
    tok_rows, width = tokens.shape
    experts = router_logits.shape[1]
    per_device = gate_weight.shape[0]
    n_expert = lax.axis_size("expert")
    n_data = lax.axis_size("dp")
    sources = n_expert * n_data
    capacity = 2 * tok_rows // experts
    slots = per_device * capacity
    slot_count = experts * capacity
    split = per_device if capacity % 16 == 0 else 1
    height = slots // split
    offset = math.log(tok_rows * sources / experts)

    route_ids = routes[:, 0]
    labels = jnp.arange(experts, dtype=jnp.int32)
    hit_table = (route_ids[:, None] == labels[None, :]).astype(jnp.int32)
    before = (jnp.arange(tok_rows)[None, :] < jnp.arange(tok_rows)[:, None]) & (
        route_ids[None, :] == route_ids[:, None]
    )
    slot_rank = jnp.sum(before.astype(jnp.int32), axis=1)
    slot_index = route_ids * capacity + slot_rank
    seat = slot_index[None, :] == jnp.arange(slot_count, dtype=jnp.int32)[:, None]
    seat_low = seat.astype(jnp.bfloat16)

    def seated(values):
        return (
            jnp.dot(seat_low, values, preferred_element_type=jnp.float32)
            .astype(jnp.bfloat16)
            .reshape(n_expert, split, height, width)
        )

    send = jnp.stack([seated(tokens), seated(d_out)], axis=1)
    logits_t = router_logits.T
    slot_logits = jnp.dot(
        logits_t, seat.astype(jnp.float32).T, precision=lax.Precision.HIGHEST
    ).reshape(experts, n_expert, slots)
    small = jnp.concatenate(
        [
            jnp.broadcast_to(logits_t[None], (n_expert, experts, tok_rows)),
            jnp.pad(slot_logits.transpose(1, 0, 2), ((0, 0), (0, 0), (0, LANES - slots))),
        ],
        axis=1,
    )
    got, small_out, row_all, col_all = dispatch(send, small, n_expert, n_data, offset)

    col_last = col_all[ITERS, :, :1]
    slot_probs = jax.nn.softmax(small_out[:, experts:, :slots] + col_last[None], axis=1)
    my_e, my_d = lax.axis_index("expert"), lax.axis_index("dp")
    slot_owner = my_e * per_device + jnp.arange(slots, dtype=jnp.int32) // capacity
    slot_chosen = (labels[:, None] == slot_owner[None, :]).astype(jnp.float32)
    slot_gating = experts * jnp.sum(slot_probs * slot_chosen[None], axis=1)
    gating_low = slot_gating.astype(jnp.bfloat16).astype(jnp.float32)

    got = got.reshape(2, split, sources, per_device // split, capacity, width)
    got = got.transpose(0, 1, 3, 2, 4, 5).reshape(2, per_device, sources * capacity, width)
    results = [
        expert_backward(
            got[0, member],
            got[1, member],
            gating_low[:, member * capacity : (member + 1) * capacity].reshape(-1),
            gate_weight[member],
            up_weight[member],
            down_weight[member],
        )
        for member in range(per_device)
    ]
    d_all = jnp.stack([outcome[0] for outcome in results], axis=0)
    d_all = d_all.reshape(split, per_device // split, sources, capacity, width)
    d_all = d_all.transpose(0, 2, 1, 3, 4).reshape(split, sources, height, width)
    d_gate_weight = jnp.stack([outcome[2] for outcome in results], axis=0)
    d_up_weight = jnp.stack([outcome[3] for outcome in results], axis=0)
    d_down_weight = jnp.stack([outcome[4] for outcome in results], axis=0)

    gating_part = jnp.concatenate(
        [outcome[1].reshape(sources, capacity) for outcome in results], axis=1
    )
    gating_part = gating_part.astype(jnp.bfloat16).astype(jnp.float32)
    first_part = jnp.sum(
        (gating_part * slot_gating)[:, None, :] * (slot_chosen[None] - slot_probs), axis=(0, 2)
    )
    tile = jnp.concatenate(
        [
            jnp.pad(gating_part, ((0, 0), (0, LANES - slots)))[:, None],
            jnp.broadcast_to(
                jnp.pad(first_part, (0, LANES - experts))[None, None], (sources, 1, LANES)
            ),
            jnp.zeros((sources, 6, LANES), jnp.float32),
        ],
        axis=1,
    )
    home, tiles, chain = collect(
        d_all, tile, small_out, row_all, col_all, n_expert, n_data, offset
    )

    d_tokens = lax.dot_general(
        seat_low,
        home.reshape(slot_count, width),
        (((0,), (0,)), ((), ())),
        preferred_element_type=jnp.float32,
    ).astype(jnp.bfloat16)
    home_gating = jnp.sum(tiles[:, 0, :slots].reshape(n_expert, n_data, slots), axis=1)
    home_gating = home_gating.astype(jnp.bfloat16).astype(jnp.float32).reshape(slot_count)
    d_gating = jnp.sum(jnp.where(seat, home_gating[:, None], 0.0), axis=0)

    me = my_e * n_data + my_d
    my_rows = lax.dynamic_index_in_dim(row_all, me, axis=1, keepdims=False)
    chosen_t = (labels[:, None] == route_ids[None, :]).astype(jnp.float32)
    probs_t = jax.nn.softmax(logits_t + col_last, axis=0)
    gating = experts * jnp.sum(probs_t * chosen_t, axis=0)
    d_logits = (d_gating * gating)[None, :] * (chosen_t - probs_t)
    for k in reversed(range(ITERS)):
        base = logits_t + my_rows[k]
        weighted = chain[k] * jnp.exp(base + col_all[k + 1] - offset)
        pulled = jnp.sum(weighted, axis=0, keepdims=True)
        d_logits = d_logits - weighted + pulled * jnp.exp(base + col_all[k])
    return (d_tokens, d_logits.T, d_gate_weight, d_up_weight, d_down_weight)


def solution(mesh):
    return jax.shard_map(
        body,
        mesh=mesh,
        in_specs=(
            P(("expert", "dp"), None),
            P(("expert", "dp"), None),
            P(("expert", "dp"), None),
            P(("expert", "dp"), None),
            P("expert", "dp", None),
            P("expert", "dp", None),
            P("expert", "dp", None),
        ),
        out_specs=(
            P(("expert", "dp"), None),
            P(("expert", "dp"), None),
            P("expert", "dp", None),
            P("expert", "dp", None),
            P("expert", "dp", None),
        ),
        check_vma=False,
    )
```

```python
import functools
import math

import jax
import jax.numpy as jnp
from jax import lax
from jax.experimental import pallas as pl
from jax.experimental.pallas import tpu as pltpu
from jax.sharding import PartitionSpec as P

ITERS = 8
LANES = 128
CHUNK = 8
WINDOW = 4
LAG = 4
EARLY = 4
Y_WINDOW = 3
ROW_TILE = 256
WIDTH_TILE = 512
MESH = pl.DeviceIdType.MESH
VMEM_LIMIT = 48 * 1024 * 1024
WIDE_LIMIT = 60 * 1024 * 1024


def place(n_expert, n_data):
    my_e, my_d = lax.axis_index("expert"), lax.axis_index("dp")
    half, core = my_d // 2, my_d % 2
    sibling = half * 2 + (1 - core)
    across = (1 - half) * 2 + core
    diagonal = (1 - half) * 2 + (1 - core)
    return my_e, my_d, half, core, sibling, across, diagonal


def partner(e, i, n_expert):
    total, weight = 0, 1
    while weight < n_expert:
        total = total + lax.rem(e // weight + i // weight, 2) * weight
        weight *= 2
    return total


def sinkhorn_step(k, offset, experts, sources, small_out, rows_out, cols_out):
    col = cols_out[k]

    def row_pass(step, top):
        at = pl.ds(step * CHUNK, CHUNK)
        logits = small_out[at, :experts, :]
        shifted = logits + col[None]
        high = jnp.max(shifted, axis=1, keepdims=True)
        row = -(high + jnp.log(jnp.sum(jnp.exp(shifted - high), axis=1, keepdims=True)))
        rows_out[k, at, :, :] = row
        return jnp.maximum(top, jnp.max(logits + row, axis=0))

    top = lax.fori_loop(
        0, sources // CHUNK, row_pass, jnp.full((experts, LANES), -1e30, jnp.float32)
    )
    top = jnp.max(top, axis=1, keepdims=True)

    def col_pass(step, total):
        at = pl.ds(step * CHUNK, CHUNK)
        logits = small_out[at, :experts, :]
        return total + jnp.sum(jnp.exp(logits + rows_out[k, at, :, :] - top[None]), axis=0)

    total = lax.fori_loop(
        0, sources // CHUNK, col_pass, jnp.zeros((experts, LANES), jnp.float32)
    )
    total = jnp.sum(total, axis=1, keepdims=True)
    cols_out[k + 1] = jnp.broadcast_to(offset - (top + jnp.log(total)), (experts, LANES))


def dispatch_kernel(
    n_expert, n_data, offset,
    send_ref, small_ref, got_ref, small_out, rows_out, cols_out,
    big_send, big_recv, small_send, small_recv, local_sem,
):
    my_e, my_d, half, core, sibling, across, diagonal = place(n_expert, n_data)
    me = my_e * n_data + my_d
    sources = n_expert * n_data
    experts = cols_out.shape[1]

    barrier = pltpu.get_barrier_semaphore()

    def greet(i, carry):
        pl.semaphore_signal(
            barrier, inc=1, device_id=(lax.rem(my_e + i, n_expert), my_d), device_id_type=MESH
        )
        return carry

    lax.fori_loop(1, n_expert, greet, 0)
    pl.semaphore_signal(barrier, inc=1, device_id=(my_e, sibling), device_id_type=MESH)
    pl.semaphore_signal(barrier, inc=1, device_id=(my_e, across), device_id_type=MESH)
    pl.semaphore_wait(barrier, n_expert + 1)

    def small_copy(src, source, leg, i, device):
        return pltpu.make_async_remote_copy(
            src_ref=src, dst_ref=small_out.at[source],
            send_sem=small_send.at[leg, i], recv_sem=small_recv.at[source],
            device_id=device, device_id_type=MESH,
        )

    pieces = 2 * (n_expert - 1)

    def flip_of(p):
        turn = p // 2
        return lax.rem(turn + 1, 2) * (n_expert // 2 + turn // 2) + lax.rem(turn, 2) * (
            1 + turn // 2
        )

    def big_copy(src, kind, source, leg, i, device):
        return pltpu.make_async_remote_copy(
            src_ref=src, dst_ref=got_ref.at[kind, :, source],
            send_sem=big_send.at[leg, kind, i], recv_sem=big_recv.at[kind, source],
            device_id=device, device_id_type=MESH,
        )

    def first_small(i, carry):
        other = lax.rem(my_e + i, n_expert)
        small_copy(small_ref.at[other], me, 0, i, (other, my_d)).start()
        return carry

    def first_big(p):
        kind, flip = lax.rem(p, 2), flip_of(p)
        other = partner(my_e, flip, n_expert)
        big_copy(send_ref.at[other, kind], kind, me, 0, flip, (other, my_d)).start()

    def first_pieces(p, carry):
        first_big(p)
        return carry

    lax.fori_loop(1, n_expert, first_small, 0)
    lax.fori_loop(0, WINDOW, first_pieces, 0)
    for kind in range(2):
        block = send_ref.at[my_e, kind]
        big_copy(block, kind, me, 1, 0, (my_e, across)).start()
        big_copy(block, kind, me, 2, 0, (my_e, sibling)).start()
    own = pltpu.make_async_copy(send_ref.at[my_e], got_ref.at[:, :, me], local_sem)
    own.start()
    small_out[me] = small_ref[my_e]
    cols_out[0] = jnp.zeros((experts, LANES), jnp.float32)

    def origin(i, lane):
        return lax.rem(my_e + n_expert - i, n_expert) * n_data + lane

    def forward_small(i, carry):
        source = origin(i, my_d)

        @pl.when(i > 0)
        def _():
            small_copy(small_out.at[source], source, 0, i, (my_e, my_d)).wait_recv()

        small_copy(small_out.at[source], source, 1, i, (my_e, across)).start()
        small_copy(small_out.at[source], source, 2, i, (my_e, sibling)).start()
        return carry

    lax.fori_loop(0, n_expert, forward_small, 0)

    def pass_on(kind, flip):
        source = partner(my_e, flip, n_expert) * n_data + my_d
        block = got_ref.at[kind, :, source]
        big_copy(block, kind, source, 1, flip, (my_e, across)).start()
        big_copy(block, kind, source, 2, flip, (my_e, sibling)).start()

    def forward_big(p):
        kind, flip = lax.rem(p, 2), flip_of(p)
        source = partner(my_e, flip, n_expert) * n_data + my_d
        big_copy(got_ref.at[kind, :, source], kind, source, 0, flip, (my_e, my_d)).wait_recv()
        pass_on(kind, flip)

    def early(p, carry):
        forward_big(p)
        first_big(p + WINDOW)
        return carry

    lax.fori_loop(0, EARLY, early, 0)

    def cross_small(i, carry):
        source = origin(i, across)
        small_copy(small_out.at[source], source, 1, i, (my_e, across)).wait_recv()
        small_copy(small_out.at[source], source, 3, i, (my_e, sibling)).start()
        return carry

    lax.fori_loop(0, n_expert, cross_small, 0)

    def last_small(i, carry):
        for lane in (sibling, diagonal):
            source = origin(i, lane)
            small_copy(small_out.at[source], source, 2, i, (my_e, sibling)).wait_recv()
        return carry

    lax.fori_loop(0, n_expert, last_small, 0)

    def cross_big(q):
        kind = lax.rem(q, 2)
        flip = jnp.where(q < 2, 0, flip_of(jnp.maximum(q - 2, 0)))
        source = partner(my_e, flip, n_expert) * n_data + across
        block = got_ref.at[kind, :, source]
        big_copy(block, kind, source, 1, flip, (my_e, across)).wait_recv()
        big_copy(block, kind, source, 3, flip, (my_e, sibling)).start()

    def step(p, carry):
        forward_big(p)

        @pl.when(p + WINDOW < pieces)
        def _():
            first_big(p + WINDOW)

        @pl.when(p >= LAG)
        def _():
            cross_big(p - LAG)

        @pl.when(p < EARLY + ITERS)
        def _():
            sinkhorn_step(p - EARLY, offset, experts, sources, small_out, rows_out, cols_out)

        return carry

    lax.fori_loop(EARLY, pieces, step, 0)
    own.wait()

    def cross_rest(q, carry):
        cross_big(q)
        return carry

    lax.fori_loop(pieces - LAG, pieces + 2, cross_rest, 0)

    def last_big(i, carry):
        for lane in (sibling, diagonal):
            source = origin(i, lane)
            for kind in range(2):
                big_copy(
                    got_ref.at[kind, :, source], kind, source, 2, i, (my_e, sibling)
                ).wait_recv()
        return carry

    lax.fori_loop(0, n_expert, last_big, 0)

    def drain(i, carry):
        def done(leg):
            small_copy(small_out.at[me], me, leg, i, (my_e, sibling)).wait_send()
            for kind in range(2):
                big_copy(
                    got_ref.at[kind, :, me], kind, me, leg, i, (my_e, sibling)
                ).wait_send()

        for leg in (1, 2, 3):
            done(leg)

        @pl.when(i > 0)
        def _():
            done(0)

        return carry

    lax.fori_loop(0, n_expert, drain, 0)


def dispatch(send, small, n_expert, n_data, offset):
    sources = n_expert * n_data
    experts = small.shape[1] // 2
    _, kinds, split, rows, width = send.shape
    return pl.pallas_call(
        functools.partial(dispatch_kernel, n_expert, n_data, offset),
        out_shape=(
            jax.ShapeDtypeStruct((kinds, split, sources, rows, width), jnp.bfloat16),
            jax.ShapeDtypeStruct((sources, 2 * experts, LANES), jnp.float32),
            jax.ShapeDtypeStruct((ITERS, sources, 1, LANES), jnp.float32),
            jax.ShapeDtypeStruct((ITERS + 1, experts, LANES), jnp.float32),
        ),
        in_specs=[pl.BlockSpec(memory_space=pl.ANY), pl.BlockSpec(memory_space=pltpu.VMEM)],
        out_specs=(
            pl.BlockSpec(memory_space=pl.ANY),
            pl.BlockSpec(memory_space=pltpu.VMEM),
            pl.BlockSpec(memory_space=pltpu.VMEM),
            pl.BlockSpec(memory_space=pltpu.VMEM),
        ),
        scratch_shapes=[
            pltpu.SemaphoreType.DMA((4, 2, n_expert)),
            pltpu.SemaphoreType.DMA((2, sources)),
            pltpu.SemaphoreType.DMA((4, n_expert)),
            pltpu.SemaphoreType.DMA((sources,)),
            pltpu.SemaphoreType.DMA,
        ],
        compiler_params=pltpu.CompilerParams(
            collective_id=0, has_side_effects=True, vmem_limit_bytes=VMEM_LIMIT
        ),
        name="dispatch",
    )(send, small)


def add_blocks(left, right):
    return (left.astype(jnp.float32) + right.astype(jnp.float32)).astype(jnp.bfloat16)


def chain_start(experts, tiles, chain_out):
    first = jnp.sum(tiles[:, 1:2, :], axis=0)
    lane = lax.broadcasted_iota(jnp.int32, (experts, LANES), 1)
    sub = lax.broadcasted_iota(jnp.int32, (experts, LANES), 0)
    spread = jnp.where(lane == sub, jnp.broadcast_to(first, (experts, LANES)), 0.0)
    d_col = jnp.sum(spread, axis=1, keepdims=True)
    chain_out[ITERS - 1] = jnp.broadcast_to(d_col, (experts, LANES))


def chain_sweep(step, offset, experts, sources, logits_ref, rows_ref, cols_ref, chain_out):
    k = ITERS - 1 - step
    d_now, col_after, col_before = chain_out[k], cols_ref[k + 1], cols_ref[k]

    def part(piece, total):
        at = pl.ds(piece * CHUNK, CHUNK)
        base = logits_ref[at, :experts, :] + rows_ref[k, at, :, :]
        pulled = jnp.sum(
            d_now[None] * jnp.exp(base + (col_after - offset)[None]), axis=1, keepdims=True
        )
        return total + jnp.sum(pulled * jnp.exp(base + col_before[None]), axis=0)

    total = lax.fori_loop(0, sources // CHUNK, part, jnp.zeros((experts, LANES), jnp.float32))
    chain_out[k - 1] = jnp.broadcast_to(jnp.sum(total, axis=1, keepdims=True), (experts, LANES))


def collect_kernel(
    n_expert, n_data, offset,
    d_ref, tile_ref, logits_ref, rows_ref, cols_ref,
    home, tiles, chain_out,
    pair, cross,
    core_send, core_recv, y_send, y_recv, home_send, home_recv, tile_send, tile_recv,
):
    my_e, my_d, half, core, sibling, across, diagonal = place(n_expert, n_data)
    me = my_e * n_data + my_d
    sources = n_expert * n_data
    experts = cols_ref.shape[1]
    other_core, other_half = 1 - core, 1 - half

    barrier = pltpu.get_barrier_semaphore()

    def peer(i):
        index = lax.rem(me + i, sources)
        return index, (index // n_data, lax.rem(index, n_data))

    def greet(i, carry):
        pl.semaphore_signal(barrier, inc=1, device_id=peer(i)[1], device_id_type=MESH)
        return carry

    lax.fori_loop(1, sources, greet, 0)
    pl.semaphore_wait(barrier, sources - 1)

    def tile_copy(i):
        index, device = peer(i)
        return pltpu.make_async_remote_copy(
            src_ref=tile_ref.at[index], dst_ref=tiles.at[me],
            send_sem=tile_send.at[i], recv_sem=tile_recv.at[me],
            device_id=device, device_id_type=MESH,
        )

    def core_copy(e, y):
        return pltpu.make_async_remote_copy(
            src_ref=d_ref.at[:, e * n_data + y * 2 + other_core], dst_ref=pair.at[:, e * 2 + y],
            send_sem=core_send.at[e * 2 + y], recv_sem=core_recv.at[e * 2 + y],
            device_id=(my_e, sibling), device_id_type=MESH,
        )

    def y_copy(e):
        return pltpu.make_async_remote_copy(
            src_ref=pair.at[:, e * 2 + other_half], dst_ref=cross.at[:, e],
            send_sem=y_send.at[e], recv_sem=y_recv.at[e],
            device_id=(my_e, across), device_id_type=MESH,
        )

    def home_copy(e):
        return pltpu.make_async_remote_copy(
            src_ref=cross.at[:, e], dst_ref=home.at[my_e],
            send_sem=home_send.at[e], recv_sem=home_recv.at[my_e],
            device_id=(e, my_d), device_id_type=MESH,
        )

    def order(i):
        half_way = n_expert // 2
        flip = jnp.where(i < half_way, i + half_way, lax.rem(i + 1 - half_way, half_way))
        return partner(my_e, flip, n_expert)

    def start_core(i, carry):
        e = order(i)
        core_copy(e, other_half).start()
        core_copy(e, half).start()
        return carry

    lax.fori_loop(0, n_expert, start_core, 0)

    def start_tile(i, carry):
        tile_copy(i).start()
        return carry

    lax.fori_loop(1, sources, start_tile, 0)
    tiles[me] = tile_ref[me]

    def fold_core(i, carry):
        e = order(i)
        away, near = e * 2 + other_half, e * 2 + half
        core_copy(e, other_half).wait_recv()
        pair[:, away] = add_blocks(pair[:, away], d_ref[:, e * n_data + other_half * 2 + core])

        @pl.when(i < Y_WINDOW)
        def _():
            y_copy(e).start()

        core_copy(e, half).wait_recv()
        pair[:, near] = add_blocks(pair[:, near], d_ref[:, e * n_data + half * 2 + core])
        return carry

    lax.fori_loop(0, n_expert, fold_core, 0)

    def tile_arrival(i, carry):
        index, device = peer(i)
        pltpu.make_async_remote_copy(
            src_ref=tile_ref.at[index], dst_ref=tiles.at[index],
            send_sem=tile_send.at[i], recv_sem=tile_recv.at[index],
            device_id=device, device_id_type=MESH,
        ).wait_recv()
        return carry

    lax.fori_loop(1, sources, tile_arrival, 0)
    chain_start(experts, tiles, chain_out)

    def sweep(step, carry):
        chain_sweep(step, offset, experts, sources, logits_ref, rows_ref, cols_ref, chain_out)
        return carry

    def fold_y(i, carry):
        e = order(i)
        y_copy(e).wait_recv()

        @pl.when(i + Y_WINDOW < n_expert)
        def _():
            y_copy(order(i + Y_WINDOW)).start()

        cross[:, e] = add_blocks(cross[:, e], pair[:, e * 2 + half])

        @pl.when(i < n_expert - 1)
        def _():
            home_copy(e).start()

        @pl.when(i < ITERS - 1)
        def _():
            sweep(i, 0)

        return carry

    lax.fori_loop(0, n_expert, fold_y, 0)
    if n_expert < ITERS - 1:
        lax.fori_loop(n_expert, ITERS - 1, sweep, 0)
    home[my_e] = cross[:, my_e]

    def home_arrival(i, carry):
        e = order(i)
        pltpu.make_async_remote_copy(
            src_ref=cross.at[:, e], dst_ref=home.at[e],
            send_sem=home_send.at[e], recv_sem=home_recv.at[e],
            device_id=(e, my_d), device_id_type=MESH,
        ).wait_recv()
        home_copy(e).wait_send()
        return carry

    lax.fori_loop(0, n_expert - 1, home_arrival, 0)

    def drain(i, carry):
        core_copy(i, 0).wait_send()
        core_copy(i, 1).wait_send()
        y_copy(i).wait_send()
        return carry

    lax.fori_loop(0, n_expert, drain, 0)

    def drain_tiles(i, carry):
        tile_copy(i).wait_send()
        return carry

    lax.fori_loop(1, sources, drain_tiles, 0)


def collect(d_all, tile, logits, rows, cols, n_expert, n_data, offset):
    split, sources, height, width = d_all.shape
    experts = cols.shape[1]
    vmem = pl.BlockSpec(memory_space=pltpu.VMEM)
    return pl.pallas_call(
        functools.partial(collect_kernel, n_expert, n_data, offset),
        out_shape=(
            jax.ShapeDtypeStruct((n_expert, split, height, width), jnp.bfloat16),
            jax.ShapeDtypeStruct(tile.shape, jnp.float32),
            jax.ShapeDtypeStruct((ITERS, experts, LANES), jnp.float32),
        ),
        in_specs=[vmem] * 5,
        out_specs=(vmem, vmem, vmem),
        scratch_shapes=[
            pltpu.VMEM((split, 2 * n_expert, height, width), jnp.bfloat16),
            pltpu.VMEM((split, n_expert, height, width), jnp.bfloat16),
            pltpu.SemaphoreType.DMA((2 * n_expert,)),
            pltpu.SemaphoreType.DMA((2 * n_expert,)),
            pltpu.SemaphoreType.DMA((n_expert,)),
            pltpu.SemaphoreType.DMA((n_expert,)),
            pltpu.SemaphoreType.DMA((n_expert,)),
            pltpu.SemaphoreType.DMA((n_expert,)),
            pltpu.SemaphoreType.DMA((sources,)),
            pltpu.SemaphoreType.DMA((sources,)),
        ],
        compiler_params=pltpu.CompilerParams(
            collective_id=1, has_side_effects=True, vmem_limit_bytes=VMEM_LIMIT
        ),
        name="collect",
    )(d_all, tile, logits, rows, cols)


def expert_kernel(got, gate, w_gate, w_up, w_down, d_rows, part, d_gate, d_up, d_down, keep):
    last_pair = (((1,), (1,)), ((), ()))
    first_pair = (((0,), (0,)), ((), ()))
    rows, width = got.shape[1], got.shape[2]

    def forward(step, carry):
        at = pl.ds(pl.multiple_of(step * ROW_TILE, ROW_TILE), ROW_TILE)
        x, dy, gate_row = got[0, at, :], got[1, at, :], gate[:, at]
        pre_gate = lax.dot_general(w_gate[...], x, last_pair, preferred_element_type=jnp.float32)
        pre_up = lax.dot_general(w_up[...], x, last_pair, preferred_element_type=jnp.float32)
        backward = lax.dot_general(w_down[...], dy, last_pair, preferred_element_type=jnp.float32)
        sigmoid = jax.nn.sigmoid(pre_gate)
        activated = pre_gate * sigmoid
        hidden = (activated * pre_up).astype(jnp.bfloat16).astype(jnp.float32)
        part[:, at] = jnp.sum(hidden * backward, axis=0, keepdims=True)
        scaled_back = backward * gate_row
        keep[0, :, at] = (
            scaled_back * pre_up * sigmoid * (1.0 + pre_gate * (1.0 - sigmoid))
        ).astype(jnp.bfloat16)
        keep[1, :, at] = (scaled_back * activated).astype(jnp.bfloat16)
        keep[2, :, at] = (hidden * gate_row).astype(jnp.bfloat16)
        return carry

    lax.fori_loop(0, rows // ROW_TILE, forward, 0)

    def products(step, carry):
        at = pl.ds(pl.multiple_of(step * WIDTH_TILE, WIDTH_TILE), WIDTH_TILE)
        x, dy = got[0, :, at], got[1, :, at]
        pre_gate, pre_up, hidden = keep[0], keep[1], keep[2]
        d_rows[:, at] = (
            lax.dot_general(pre_gate, w_gate[:, at], first_pair, preferred_element_type=jnp.float32)
            + lax.dot_general(pre_up, w_up[:, at], first_pair, preferred_element_type=jnp.float32)
        ).astype(jnp.bfloat16)
        d_gate[:, at] = jnp.dot(pre_gate, x, preferred_element_type=jnp.float32).astype(jnp.bfloat16)
        d_up[:, at] = jnp.dot(pre_up, x, preferred_element_type=jnp.float32).astype(jnp.bfloat16)
        d_down[:, at] = jnp.dot(hidden, dy, preferred_element_type=jnp.float32).astype(jnp.bfloat16)
        return carry

    lax.fori_loop(0, width // WIDTH_TILE, products, 0)


def expert_backward(got, gate, gate_weight, up_weight, down_weight):
    _, members, rows, width = got.shape
    units = gate_weight.shape[1]
    rows_spec = pl.BlockSpec((2, None, rows, width), lambda m: (0, m, 0, 0))
    row_spec = pl.BlockSpec((None, 1, rows), lambda m: (m, 0, 0))
    weight_spec = pl.BlockSpec((None, units, width), lambda m: (m, 0, 0))
    weight_shape = jax.ShapeDtypeStruct((members, units, width), jnp.bfloat16)
    return pl.pallas_call(
        expert_kernel,
        grid=(members,),
        out_shape=(
            jax.ShapeDtypeStruct((members, rows, width), jnp.bfloat16),
            jax.ShapeDtypeStruct((members, 1, rows), jnp.float32),
            weight_shape,
            weight_shape,
            weight_shape,
        ),
        in_specs=[rows_spec, row_spec, weight_spec, weight_spec, weight_spec],
        out_specs=(
            pl.BlockSpec((None, rows, width), lambda m: (m, 0, 0)),
            row_spec,
            weight_spec,
            weight_spec,
            weight_spec,
        ),
        scratch_shapes=[pltpu.VMEM((3, units, rows), jnp.bfloat16)],
        compiler_params=pltpu.CompilerParams(vmem_limit_bytes=WIDE_LIMIT),
        name="experts",
    )(got, gate, gate_weight, up_weight, down_weight)


def body(tokens, d_out, router_logits, routes, gate_weight, up_weight, down_weight):
    tok_rows, width = tokens.shape
    experts = router_logits.shape[1]
    per_device = gate_weight.shape[0]
    n_expert = lax.axis_size("expert")
    n_data = lax.axis_size("dp")
    sources = n_expert * n_data
    capacity = 2 * tok_rows // experts
    slots = per_device * capacity
    slot_count = experts * capacity
    split = per_device if capacity % 16 == 0 else 1
    height = slots // split
    offset = math.log(tok_rows * sources / experts)

    route_ids = routes[:, 0]
    labels = jnp.arange(experts, dtype=jnp.int32)
    hit_table = (route_ids[:, None] == labels[None, :]).astype(jnp.int32)
    before = (jnp.arange(tok_rows)[None, :] < jnp.arange(tok_rows)[:, None]) & (
        route_ids[None, :] == route_ids[:, None]
    )
    slot_rank = jnp.sum(before.astype(jnp.int32), axis=1)
    slot_index = route_ids * capacity + slot_rank
    seat = slot_index[None, :] == jnp.arange(slot_count, dtype=jnp.int32)[:, None]
    seat_low = seat.astype(jnp.bfloat16)

    def seated(values):
        return (
            jnp.dot(seat_low, values, preferred_element_type=jnp.float32)
            .astype(jnp.bfloat16)
            .reshape(n_expert, split, height, width)
        )

    send = jnp.stack([seated(tokens), seated(d_out)], axis=1)
    logits_t = router_logits.T
    slot_logits = jnp.dot(
        logits_t, seat.astype(jnp.float32).T, precision=lax.Precision.HIGHEST
    ).reshape(experts, n_expert, slots)
    small = jnp.concatenate(
        [
            jnp.broadcast_to(logits_t[None], (n_expert, experts, tok_rows)),
            jnp.pad(slot_logits.transpose(1, 0, 2), ((0, 0), (0, 0), (0, LANES - slots))),
        ],
        axis=1,
    )
    got, small_out, row_all, col_all = dispatch(send, small, n_expert, n_data, offset)

    col_last = col_all[ITERS, :, :1]
    slot_probs = jax.nn.softmax(small_out[:, experts:, :slots] + col_last[None], axis=1)
    my_e, my_d = lax.axis_index("expert"), lax.axis_index("dp")
    slot_owner = my_e * per_device + jnp.arange(slots, dtype=jnp.int32) // capacity
    slot_chosen = (labels[:, None] == slot_owner[None, :]).astype(jnp.float32)
    slot_gating = experts * jnp.sum(slot_probs * slot_chosen[None], axis=1)
    gating_low = slot_gating.astype(jnp.bfloat16).astype(jnp.float32)

    got = got.reshape(2, split, sources, per_device // split, capacity, width)
    got = got.transpose(0, 1, 3, 2, 4, 5).reshape(2, per_device, sources * capacity, width)
    gate_rows = gating_low.reshape(sources, per_device, capacity).transpose(1, 0, 2)
    d_all, gating_part, d_gate_weight, d_up_weight, d_down_weight = expert_backward(
        got,
        gate_rows.reshape(per_device, 1, sources * capacity),
        gate_weight,
        up_weight,
        down_weight,
    )
    d_all = d_all.reshape(split, per_device // split, sources, capacity, width)
    d_all = d_all.transpose(0, 2, 1, 3, 4).reshape(split, sources, height, width)
    gating_part = gating_part.reshape(per_device, sources, capacity).transpose(1, 0, 2)
    gating_part = gating_part.reshape(sources, slots)
    gating_part = gating_part.astype(jnp.bfloat16).astype(jnp.float32)
    first_part = jnp.sum(
        (gating_part * slot_gating)[:, None, :] * (slot_chosen[None] - slot_probs), axis=(0, 2)
    )
    tile = jnp.concatenate(
        [
            jnp.pad(gating_part, ((0, 0), (0, LANES - slots)))[:, None],
            jnp.broadcast_to(
                jnp.pad(first_part, (0, LANES - experts))[None, None], (sources, 1, LANES)
            ),
            jnp.zeros((sources, 6, LANES), jnp.float32),
        ],
        axis=1,
    )
    home, tiles, chain = collect(
        d_all, tile, small_out, row_all, col_all, n_expert, n_data, offset
    )

    d_tokens = lax.dot_general(
        seat_low,
        home.reshape(slot_count, width),
        (((0,), (0,)), ((), ())),
        preferred_element_type=jnp.float32,
    ).astype(jnp.bfloat16)
    home_gating = jnp.sum(tiles[:, 0, :slots].reshape(n_expert, n_data, slots), axis=1)
    home_gating = home_gating.astype(jnp.bfloat16).astype(jnp.float32).reshape(slot_count)
    d_gating = jnp.sum(jnp.where(seat, home_gating[:, None], 0.0), axis=0)

    me = my_e * n_data + my_d
    my_rows = lax.dynamic_index_in_dim(row_all, me, axis=1, keepdims=False)
    chosen_t = (labels[:, None] == route_ids[None, :]).astype(jnp.float32)
    probs_t = jax.nn.softmax(logits_t + col_last, axis=0)
    gating = experts * jnp.sum(probs_t * chosen_t, axis=0)
    d_logits = (d_gating * gating)[None, :] * (chosen_t - probs_t)
    for k in reversed(range(ITERS)):
        base = logits_t + my_rows[k]
        weighted = chain[k] * jnp.exp(base + col_all[k + 1] - offset)
        pulled = jnp.sum(weighted, axis=0, keepdims=True)
        d_logits = d_logits - weighted + pulled * jnp.exp(base + col_all[k])
    return (d_tokens, d_logits.T, d_gate_weight, d_up_weight, d_down_weight)


def solution(mesh):
    return jax.shard_map(
        body,
        mesh=mesh,
        in_specs=(
            P(("expert", "dp"), None),
            P(("expert", "dp"), None),
            P(("expert", "dp"), None),
            P(("expert", "dp"), None),
            P("expert", "dp", None),
            P("expert", "dp", None),
            P("expert", "dp", None),
        ),
        out_specs=(
            P(("expert", "dp"), None),
            P(("expert", "dp"), None),
            P("expert", "dp", None),
            P("expert", "dp", None),
            P("expert", "dp", None),
        ),
        check_vma=False,
    )
```

```python
import functools
import math

import jax
import jax.numpy as jnp
from jax import lax
from jax.experimental import pallas as pl
from jax.experimental.pallas import tpu as pltpu
from jax.sharding import PartitionSpec as P

ITERS = 8
LANES = 128
CHUNK = 8
WINDOW = 4
LAG = 4
EARLY = 4
Y_WINDOW = 3
ROW_TILE = 256
WIDTH_TILE = 512
MESH = pl.DeviceIdType.MESH
VMEM_LIMIT = 48 * 1024 * 1024
WIDE_LIMIT = 60 * 1024 * 1024


def place(n_expert, n_data):
    my_e, my_d = lax.axis_index("expert"), lax.axis_index("dp")
    half, core = my_d // 2, my_d % 2
    sibling = half * 2 + (1 - core)
    across = (1 - half) * 2 + core
    diagonal = (1 - half) * 2 + (1 - core)
    return my_e, my_d, half, core, sibling, across, diagonal


def partner(e, i, n_expert):
    total, weight = 0, 1
    while weight < n_expert:
        total = total + lax.rem(e // weight + i // weight, 2) * weight
        weight *= 2
    return total


def sinkhorn_step(k, offset, experts, sources, small_out, rows_out, cols_out):
    col = cols_out[k]

    def row_pass(step, top):
        at = pl.ds(step * CHUNK, CHUNK)
        logits = small_out[at, :experts, :]
        shifted = logits + col[None]
        high = jnp.max(shifted, axis=1, keepdims=True)
        row = -(high + jnp.log(jnp.sum(jnp.exp(shifted - high), axis=1, keepdims=True)))
        rows_out[k, at, :, :] = row
        return jnp.maximum(top, jnp.max(logits + row, axis=0))

    top = lax.fori_loop(
        0, sources // CHUNK, row_pass, jnp.full((experts, LANES), -1e30, jnp.float32)
    )
    top = jnp.max(top, axis=1, keepdims=True)

    def col_pass(step, total):
        at = pl.ds(step * CHUNK, CHUNK)
        logits = small_out[at, :experts, :]
        return total + jnp.sum(jnp.exp(logits + rows_out[k, at, :, :] - top[None]), axis=0)

    total = lax.fori_loop(
        0, sources // CHUNK, col_pass, jnp.zeros((experts, LANES), jnp.float32)
    )
    total = jnp.sum(total, axis=1, keepdims=True)
    cols_out[k + 1] = jnp.broadcast_to(offset - (top + jnp.log(total)), (experts, LANES))


def dispatch_kernel(
    n_expert, n_data, offset,
    send_ref, small_ref, got_ref, small_out, rows_out, cols_out,
    big_send, big_recv, small_send, small_recv, local_sem,
):
    my_e, my_d, half, core, sibling, across, diagonal = place(n_expert, n_data)
    me = my_e * n_data + my_d
    sources = n_expert * n_data
    experts = cols_out.shape[1]

    barrier = pltpu.get_barrier_semaphore()

    def greet(i, carry):
        pl.semaphore_signal(
            barrier, inc=1, device_id=(lax.rem(my_e + i, n_expert), my_d), device_id_type=MESH
        )
        return carry

    lax.fori_loop(1, n_expert, greet, 0)
    pl.semaphore_signal(barrier, inc=1, device_id=(my_e, sibling), device_id_type=MESH)
    pl.semaphore_signal(barrier, inc=1, device_id=(my_e, across), device_id_type=MESH)
    pl.semaphore_wait(barrier, n_expert + 1)

    def small_copy(src, source, leg, i, device):
        return pltpu.make_async_remote_copy(
            src_ref=src, dst_ref=small_out.at[source],
            send_sem=small_send.at[leg, i], recv_sem=small_recv.at[source],
            device_id=device, device_id_type=MESH,
        )

    pieces = 2 * (n_expert - 1)

    def flip_of(p):
        turn = p // 2
        return lax.rem(turn + 1, 2) * (n_expert // 2 + turn // 2) + lax.rem(turn, 2) * (
            1 + turn // 2
        )

    def big_copy(src, kind, source, leg, i, device):
        return pltpu.make_async_remote_copy(
            src_ref=src, dst_ref=got_ref.at[kind, :, source],
            send_sem=big_send.at[leg, kind, i], recv_sem=big_recv.at[kind, source],
            device_id=device, device_id_type=MESH,
        )

    def first_small(i, carry):
        other = lax.rem(my_e + i, n_expert)
        small_copy(small_ref.at[other], me, 0, i, (other, my_d)).start()
        return carry

    def first_big(p):
        kind, flip = lax.rem(p, 2), flip_of(p)
        other = partner(my_e, flip, n_expert)
        big_copy(send_ref.at[other, kind], kind, me, 0, flip, (other, my_d)).start()

    def first_pieces(p, carry):
        first_big(p)
        return carry

    lax.fori_loop(1, n_expert, first_small, 0)
    lax.fori_loop(0, WINDOW, first_pieces, 0)
    for kind in range(2):
        block = send_ref.at[my_e, kind]
        big_copy(block, kind, me, 1, 0, (my_e, across)).start()
        big_copy(block, kind, me, 2, 0, (my_e, sibling)).start()
    own = pltpu.make_async_copy(send_ref.at[my_e], got_ref.at[:, :, me], local_sem)
    own.start()
    small_out[me] = small_ref[my_e]
    cols_out[0] = jnp.zeros((experts, LANES), jnp.float32)

    def origin(i, lane):
        return lax.rem(my_e + n_expert - i, n_expert) * n_data + lane

    def forward_small(i, carry):
        source = origin(i, my_d)

        @pl.when(i > 0)
        def _():
            small_copy(small_out.at[source], source, 0, i, (my_e, my_d)).wait_recv()

        small_copy(small_out.at[source], source, 1, i, (my_e, across)).start()
        small_copy(small_out.at[source], source, 2, i, (my_e, sibling)).start()
        return carry

    lax.fori_loop(0, n_expert, forward_small, 0)

    def pass_on(kind, flip):
        source = partner(my_e, flip, n_expert) * n_data + my_d
        block = got_ref.at[kind, :, source]
        big_copy(block, kind, source, 1, flip, (my_e, across)).start()
        big_copy(block, kind, source, 2, flip, (my_e, sibling)).start()

    def forward_big(p):
        kind, flip = lax.rem(p, 2), flip_of(p)
        source = partner(my_e, flip, n_expert) * n_data + my_d
        big_copy(got_ref.at[kind, :, source], kind, source, 0, flip, (my_e, my_d)).wait_recv()
        pass_on(kind, flip)

    def early(p, carry):
        forward_big(p)
        first_big(p + WINDOW)
        return carry

    lax.fori_loop(0, EARLY, early, 0)

    def cross_small(i, carry):
        source = origin(i, across)
        small_copy(small_out.at[source], source, 1, i, (my_e, across)).wait_recv()
        small_copy(small_out.at[source], source, 3, i, (my_e, sibling)).start()
        return carry

    lax.fori_loop(0, n_expert, cross_small, 0)

    def last_small(i, carry):
        for lane in (sibling, diagonal):
            source = origin(i, lane)
            small_copy(small_out.at[source], source, 2, i, (my_e, sibling)).wait_recv()
        return carry

    lax.fori_loop(0, n_expert, last_small, 0)

    def cross_big(q):
        kind = lax.rem(q, 2)
        flip = jnp.where(q < 2, 0, flip_of(jnp.maximum(q - 2, 0)))
        source = partner(my_e, flip, n_expert) * n_data + across
        block = got_ref.at[kind, :, source]
        big_copy(block, kind, source, 1, flip, (my_e, across)).wait_recv()
        big_copy(block, kind, source, 3, flip, (my_e, sibling)).start()

    def step(p, carry):
        forward_big(p)

        @pl.when(p + WINDOW < pieces)
        def _():
            first_big(p + WINDOW)

        @pl.when(p >= LAG)
        def _():
            cross_big(p - LAG)

        @pl.when(p < EARLY + ITERS)
        def _():
            sinkhorn_step(p - EARLY, offset, experts, sources, small_out, rows_out, cols_out)

        return carry

    lax.fori_loop(EARLY, pieces, step, 0)
    own.wait()

    def cross_rest(q, carry):
        cross_big(q)
        return carry

    lax.fori_loop(pieces - LAG, pieces + 2, cross_rest, 0)

    def last_big(i, carry):
        for lane in (sibling, diagonal):
            source = origin(i, lane)
            for kind in range(2):
                big_copy(
                    got_ref.at[kind, :, source], kind, source, 2, i, (my_e, sibling)
                ).wait_recv()
        return carry

    lax.fori_loop(0, n_expert, last_big, 0)

    def drain(i, carry):
        def done(leg):
            small_copy(small_out.at[me], me, leg, i, (my_e, sibling)).wait_send()
            for kind in range(2):
                big_copy(
                    got_ref.at[kind, :, me], kind, me, leg, i, (my_e, sibling)
                ).wait_send()

        for leg in (1, 2, 3):
            done(leg)

        @pl.when(i > 0)
        def _():
            done(0)

        return carry

    lax.fori_loop(0, n_expert, drain, 0)


def dispatch(send, small, n_expert, n_data, offset):
    sources = n_expert * n_data
    experts = small.shape[1] // 2
    _, kinds, split, rows, width = send.shape
    return pl.pallas_call(
        functools.partial(dispatch_kernel, n_expert, n_data, offset),
        out_shape=(
            jax.ShapeDtypeStruct((kinds, split, sources, rows, width), jnp.bfloat16),
            jax.ShapeDtypeStruct((sources, 2 * experts, LANES), jnp.float32),
            jax.ShapeDtypeStruct((ITERS, sources, 1, LANES), jnp.float32),
            jax.ShapeDtypeStruct((ITERS + 1, experts, LANES), jnp.float32),
        ),
        in_specs=[pl.BlockSpec(memory_space=pl.ANY), pl.BlockSpec(memory_space=pltpu.VMEM)],
        out_specs=(
            pl.BlockSpec(memory_space=pl.ANY),
            pl.BlockSpec(memory_space=pltpu.VMEM),
            pl.BlockSpec(memory_space=pltpu.VMEM),
            pl.BlockSpec(memory_space=pltpu.VMEM),
        ),
        scratch_shapes=[
            pltpu.SemaphoreType.DMA((4, 2, n_expert)),
            pltpu.SemaphoreType.DMA((2, sources)),
            pltpu.SemaphoreType.DMA((4, n_expert)),
            pltpu.SemaphoreType.DMA((sources,)),
            pltpu.SemaphoreType.DMA,
        ],
        compiler_params=pltpu.CompilerParams(
            collective_id=0, has_side_effects=True, vmem_limit_bytes=VMEM_LIMIT
        ),
        name="dispatch",
    )(send, small)


def add_blocks(left, right):
    return (left.astype(jnp.float32) + right.astype(jnp.float32)).astype(jnp.bfloat16)


def chain_start(experts, tiles, chain_out):
    first = jnp.sum(tiles[:, 1:2, :], axis=0)
    lane = lax.broadcasted_iota(jnp.int32, (experts, LANES), 1)
    sub = lax.broadcasted_iota(jnp.int32, (experts, LANES), 0)
    spread = jnp.where(lane == sub, jnp.broadcast_to(first, (experts, LANES)), 0.0)
    d_col = jnp.sum(spread, axis=1, keepdims=True)
    chain_out[ITERS - 1] = jnp.broadcast_to(d_col, (experts, LANES))


def chain_sweep(step, offset, experts, sources, logits_ref, rows_ref, cols_ref, chain_out):
    k = ITERS - 1 - step
    d_now, col_after, col_before = chain_out[k], cols_ref[k + 1], cols_ref[k]

    def part(piece, total):
        at = pl.ds(piece * CHUNK, CHUNK)
        base = logits_ref[at, :experts, :] + rows_ref[k, at, :, :]
        pulled = jnp.sum(
            d_now[None] * jnp.exp(base + (col_after - offset)[None]), axis=1, keepdims=True
        )
        return total + jnp.sum(pulled * jnp.exp(base + col_before[None]), axis=0)

    total = lax.fori_loop(0, sources // CHUNK, part, jnp.zeros((experts, LANES), jnp.float32))
    chain_out[k - 1] = jnp.broadcast_to(jnp.sum(total, axis=1, keepdims=True), (experts, LANES))


def collect_kernel(
    n_expert, n_data, offset,
    d_ref, tile_ref, logits_ref, rows_ref, cols_ref,
    home, tiles, chain_out,
    pair, cross,
    core_send, core_recv, y_send, y_recv, home_send, home_recv, tile_send, tile_recv,
):
    my_e, my_d, half, core, sibling, across, diagonal = place(n_expert, n_data)
    me = my_e * n_data + my_d
    sources = n_expert * n_data
    experts = cols_ref.shape[1]
    other_core, other_half = 1 - core, 1 - half

    barrier = pltpu.get_barrier_semaphore()

    def peer(i):
        index = lax.rem(me + i, sources)
        return index, (index // n_data, lax.rem(index, n_data))

    def greet(i, carry):
        pl.semaphore_signal(barrier, inc=1, device_id=peer(i)[1], device_id_type=MESH)
        return carry

    lax.fori_loop(1, sources, greet, 0)
    pl.semaphore_wait(barrier, sources - 1)

    def tile_copy(i):
        index, device = peer(i)
        return pltpu.make_async_remote_copy(
            src_ref=tile_ref.at[index], dst_ref=tiles.at[me],
            send_sem=tile_send.at[i], recv_sem=tile_recv.at[me],
            device_id=device, device_id_type=MESH,
        )

    def core_copy(e, y):
        return pltpu.make_async_remote_copy(
            src_ref=d_ref.at[:, e * n_data + y * 2 + other_core], dst_ref=pair.at[:, e * 2 + y],
            send_sem=core_send.at[e * 2 + y], recv_sem=core_recv.at[e * 2 + y],
            device_id=(my_e, sibling), device_id_type=MESH,
        )

    def y_copy(e):
        return pltpu.make_async_remote_copy(
            src_ref=pair.at[:, e * 2 + other_half], dst_ref=cross.at[:, e],
            send_sem=y_send.at[e], recv_sem=y_recv.at[e],
            device_id=(my_e, across), device_id_type=MESH,
        )

    def home_copy(e):
        return pltpu.make_async_remote_copy(
            src_ref=cross.at[:, e], dst_ref=home.at[my_e],
            send_sem=home_send.at[e], recv_sem=home_recv.at[my_e],
            device_id=(e, my_d), device_id_type=MESH,
        )

    def order(i):
        half_way = n_expert // 2
        flip = jnp.where(i < half_way, i + half_way, lax.rem(i + 1 - half_way, half_way))
        return partner(my_e, flip, n_expert)

    def start_away(i, carry):
        core_copy(order(i), other_half).start()
        return carry

    def start_near(i, carry):
        core_copy(order(i), half).start()
        return carry

    lax.fori_loop(0, n_expert, start_away, 0)
    lax.fori_loop(0, n_expert, start_near, 0)

    def start_tile(i, carry):
        tile_copy(i).start()
        return carry

    lax.fori_loop(1, sources, start_tile, 0)
    tiles[me] = tile_ref[me]

    def fold_core(i, carry):
        e = order(i)
        away = e * 2 + other_half
        core_copy(e, other_half).wait_recv()
        pair[:, away] = add_blocks(pair[:, away], d_ref[:, e * n_data + other_half * 2 + core])

        @pl.when(i < Y_WINDOW)
        def _():
            y_copy(e).start()

        return carry

    lax.fori_loop(0, n_expert, fold_core, 0)

    def tile_arrival(i, carry):
        index, device = peer(i)
        pltpu.make_async_remote_copy(
            src_ref=tile_ref.at[index], dst_ref=tiles.at[index],
            send_sem=tile_send.at[i], recv_sem=tile_recv.at[index],
            device_id=device, device_id_type=MESH,
        ).wait_recv()
        return carry

    lax.fori_loop(1, sources, tile_arrival, 0)
    chain_start(experts, tiles, chain_out)

    def sweep(step, carry):
        chain_sweep(step, offset, experts, sources, logits_ref, rows_ref, cols_ref, chain_out)
        return carry

    def fold_y(i, carry):
        e = order(i)
        y_copy(e).wait_recv()

        @pl.when(i + Y_WINDOW < n_expert)
        def _():
            y_copy(order(i + Y_WINDOW)).start()

        core_copy(e, half).wait_recv()
        own_sum = pair[:, e * 2 + half].astype(jnp.float32) + d_ref[
            :, e * n_data + half * 2 + core
        ].astype(jnp.float32)
        cross[:, e] = (cross[:, e].astype(jnp.float32) + own_sum).astype(jnp.bfloat16)

        @pl.when(i < n_expert - 1)
        def _():
            home_copy(e).start()

        @pl.when(i < ITERS - 1)
        def _():
            sweep(i, 0)

        return carry

    lax.fori_loop(0, n_expert, fold_y, 0)
    if n_expert < ITERS - 1:
        lax.fori_loop(n_expert, ITERS - 1, sweep, 0)
    home[my_e] = cross[:, my_e]

    def home_arrival(i, carry):
        e = order(i)
        pltpu.make_async_remote_copy(
            src_ref=cross.at[:, e], dst_ref=home.at[e],
            send_sem=home_send.at[e], recv_sem=home_recv.at[e],
            device_id=(e, my_d), device_id_type=MESH,
        ).wait_recv()
        home_copy(e).wait_send()
        return carry

    lax.fori_loop(0, n_expert - 1, home_arrival, 0)

    def drain(i, carry):
        core_copy(i, 0).wait_send()
        core_copy(i, 1).wait_send()
        y_copy(i).wait_send()
        return carry

    lax.fori_loop(0, n_expert, drain, 0)

    def drain_tiles(i, carry):
        tile_copy(i).wait_send()
        return carry

    lax.fori_loop(1, sources, drain_tiles, 0)


def collect(d_all, tile, logits, rows, cols, n_expert, n_data, offset):
    split, sources, height, width = d_all.shape
    experts = cols.shape[1]
    vmem = pl.BlockSpec(memory_space=pltpu.VMEM)
    return pl.pallas_call(
        functools.partial(collect_kernel, n_expert, n_data, offset),
        out_shape=(
            jax.ShapeDtypeStruct((n_expert, split, height, width), jnp.bfloat16),
            jax.ShapeDtypeStruct(tile.shape, jnp.float32),
            jax.ShapeDtypeStruct((ITERS, experts, LANES), jnp.float32),
        ),
        in_specs=[vmem] * 5,
        out_specs=(vmem, vmem, vmem),
        scratch_shapes=[
            pltpu.VMEM((split, 2 * n_expert, height, width), jnp.bfloat16),
            pltpu.VMEM((split, n_expert, height, width), jnp.bfloat16),
            pltpu.SemaphoreType.DMA((2 * n_expert,)),
            pltpu.SemaphoreType.DMA((2 * n_expert,)),
            pltpu.SemaphoreType.DMA((n_expert,)),
            pltpu.SemaphoreType.DMA((n_expert,)),
            pltpu.SemaphoreType.DMA((n_expert,)),
            pltpu.SemaphoreType.DMA((n_expert,)),
            pltpu.SemaphoreType.DMA((sources,)),
            pltpu.SemaphoreType.DMA((sources,)),
        ],
        compiler_params=pltpu.CompilerParams(
            collective_id=1, has_side_effects=True, vmem_limit_bytes=VMEM_LIMIT
        ),
        name="collect",
    )(d_all, tile, logits, rows, cols)


def expert_kernel(got, gate, w_gate, w_up, w_down, d_rows, part, d_gate, d_up, d_down, keep):
    last_pair = (((1,), (1,)), ((), ()))
    first_pair = (((0,), (0,)), ((), ()))
    rows, width = got.shape[1], got.shape[2]

    def forward(step, carry):
        at = pl.ds(pl.multiple_of(step * ROW_TILE, ROW_TILE), ROW_TILE)
        x, dy, gate_row = got[0, at, :], got[1, at, :], gate[:, at]
        pre_gate = lax.dot_general(w_gate[...], x, last_pair, preferred_element_type=jnp.float32)
        pre_up = lax.dot_general(w_up[...], x, last_pair, preferred_element_type=jnp.float32)
        backward = lax.dot_general(w_down[...], dy, last_pair, preferred_element_type=jnp.float32)
        sigmoid = jax.nn.sigmoid(pre_gate)
        activated = pre_gate * sigmoid
        hidden = (activated * pre_up).astype(jnp.bfloat16).astype(jnp.float32)
        part[:, at] = jnp.sum(hidden * backward, axis=0, keepdims=True)
        scaled_back = backward * gate_row
        keep[0, :, at] = (
            scaled_back * pre_up * sigmoid * (1.0 + pre_gate * (1.0 - sigmoid))
        ).astype(jnp.bfloat16)
        keep[1, :, at] = (scaled_back * activated).astype(jnp.bfloat16)
        keep[2, :, at] = (hidden * gate_row).astype(jnp.bfloat16)
        return carry

    lax.fori_loop(0, rows // ROW_TILE, forward, 0)

    def products(step, carry):
        at = pl.ds(pl.multiple_of(step * WIDTH_TILE, WIDTH_TILE), WIDTH_TILE)
        x, dy = got[0, :, at], got[1, :, at]
        pre_gate, pre_up, hidden = keep[0], keep[1], keep[2]
        d_rows[:, at] = (
            lax.dot_general(pre_gate, w_gate[:, at], first_pair, preferred_element_type=jnp.float32)
            + lax.dot_general(pre_up, w_up[:, at], first_pair, preferred_element_type=jnp.float32)
        ).astype(jnp.bfloat16)
        d_gate[:, at] = jnp.dot(pre_gate, x, preferred_element_type=jnp.float32).astype(jnp.bfloat16)
        d_up[:, at] = jnp.dot(pre_up, x, preferred_element_type=jnp.float32).astype(jnp.bfloat16)
        d_down[:, at] = jnp.dot(hidden, dy, preferred_element_type=jnp.float32).astype(jnp.bfloat16)
        return carry

    lax.fori_loop(0, width // WIDTH_TILE, products, 0)


def expert_backward(got, gate, gate_weight, up_weight, down_weight):
    _, members, rows, width = got.shape
    units = gate_weight.shape[1]
    rows_spec = pl.BlockSpec((2, None, rows, width), lambda m: (0, m, 0, 0))
    row_spec = pl.BlockSpec((None, 1, rows), lambda m: (m, 0, 0))
    weight_spec = pl.BlockSpec((None, units, width), lambda m: (m, 0, 0))
    weight_shape = jax.ShapeDtypeStruct((members, units, width), jnp.bfloat16)
    return pl.pallas_call(
        expert_kernel,
        grid=(members,),
        out_shape=(
            jax.ShapeDtypeStruct((members, rows, width), jnp.bfloat16),
            jax.ShapeDtypeStruct((members, 1, rows), jnp.float32),
            weight_shape,
            weight_shape,
            weight_shape,
        ),
        in_specs=[rows_spec, row_spec, weight_spec, weight_spec, weight_spec],
        out_specs=(
            pl.BlockSpec((None, rows, width), lambda m: (m, 0, 0)),
            row_spec,
            weight_spec,
            weight_spec,
            weight_spec,
        ),
        scratch_shapes=[pltpu.VMEM((3, units, rows), jnp.bfloat16)],
        compiler_params=pltpu.CompilerParams(vmem_limit_bytes=WIDE_LIMIT),
        name="experts",
    )(got, gate, gate_weight, up_weight, down_weight)


def body(tokens, d_out, router_logits, routes, gate_weight, up_weight, down_weight):
    tok_rows, width = tokens.shape
    experts = router_logits.shape[1]
    per_device = gate_weight.shape[0]
    n_expert = lax.axis_size("expert")
    n_data = lax.axis_size("dp")
    sources = n_expert * n_data
    capacity = 2 * tok_rows // experts
    slots = per_device * capacity
    slot_count = experts * capacity
    split = per_device if capacity % 16 == 0 else 1
    height = slots // split
    offset = math.log(tok_rows * sources / experts)

    route_ids = routes[:, 0]
    labels = jnp.arange(experts, dtype=jnp.int32)
    hit_table = (route_ids[:, None] == labels[None, :]).astype(jnp.int32)
    before = (jnp.arange(tok_rows)[None, :] < jnp.arange(tok_rows)[:, None]) & (
        route_ids[None, :] == route_ids[:, None]
    )
    slot_rank = jnp.sum(before.astype(jnp.int32), axis=1)
    slot_index = route_ids * capacity + slot_rank
    seat = slot_index[None, :] == jnp.arange(slot_count, dtype=jnp.int32)[:, None]
    seat_low = seat.astype(jnp.bfloat16)

    def seated(values):
        return (
            jnp.dot(seat_low, values, preferred_element_type=jnp.float32)
            .astype(jnp.bfloat16)
            .reshape(n_expert, split, height, width)
        )

    send = jnp.stack([seated(tokens), seated(d_out)], axis=1)
    logits_t = router_logits.T
    slot_logits = jnp.dot(
        logits_t, seat.astype(jnp.float32).T, precision=lax.Precision.HIGHEST
    ).reshape(experts, n_expert, slots)
    small = jnp.concatenate(
        [
            jnp.broadcast_to(logits_t[None], (n_expert, experts, tok_rows)),
            jnp.pad(slot_logits.transpose(1, 0, 2), ((0, 0), (0, 0), (0, LANES - slots))),
        ],
        axis=1,
    )
    got, small_out, row_all, col_all = dispatch(send, small, n_expert, n_data, offset)

    col_last = col_all[ITERS, :, :1]
    slot_probs = jax.nn.softmax(small_out[:, experts:, :slots] + col_last[None], axis=1)
    my_e, my_d = lax.axis_index("expert"), lax.axis_index("dp")
    slot_owner = my_e * per_device + jnp.arange(slots, dtype=jnp.int32) // capacity
    slot_chosen = (labels[:, None] == slot_owner[None, :]).astype(jnp.float32)
    slot_gating = experts * jnp.sum(slot_probs * slot_chosen[None], axis=1)
    gating_low = slot_gating.astype(jnp.bfloat16).astype(jnp.float32)

    got = got.reshape(2, split, sources, per_device // split, capacity, width)
    got = got.transpose(0, 1, 3, 2, 4, 5).reshape(2, per_device, sources * capacity, width)
    gate_rows = gating_low.reshape(sources, per_device, capacity).transpose(1, 0, 2)
    d_all, gating_part, d_gate_weight, d_up_weight, d_down_weight = expert_backward(
        got,
        gate_rows.reshape(per_device, 1, sources * capacity),
        gate_weight,
        up_weight,
        down_weight,
    )
    d_all = d_all.reshape(split, per_device // split, sources, capacity, width)
    d_all = d_all.transpose(0, 2, 1, 3, 4).reshape(split, sources, height, width)
    gating_part = gating_part.reshape(per_device, sources, capacity).transpose(1, 0, 2)
    gating_part = gating_part.reshape(sources, slots)
    gating_part = gating_part.astype(jnp.bfloat16).astype(jnp.float32)
    first_part = jnp.sum(
        (gating_part * slot_gating)[:, None, :] * (slot_chosen[None] - slot_probs), axis=(0, 2)
    )
    tile = jnp.concatenate(
        [
            jnp.pad(gating_part, ((0, 0), (0, LANES - slots)))[:, None],
            jnp.broadcast_to(
                jnp.pad(first_part, (0, LANES - experts))[None, None], (sources, 1, LANES)
            ),
            jnp.zeros((sources, 6, LANES), jnp.float32),
        ],
        axis=1,
    )
    home, tiles, chain = collect(
        d_all, tile, small_out, row_all, col_all, n_expert, n_data, offset
    )

    d_tokens = lax.dot_general(
        seat_low,
        home.reshape(slot_count, width),
        (((0,), (0,)), ((), ())),
        preferred_element_type=jnp.float32,
    ).astype(jnp.bfloat16)
    home_gating = jnp.sum(tiles[:, 0, :slots].reshape(n_expert, n_data, slots), axis=1)
    home_gating = home_gating.astype(jnp.bfloat16).astype(jnp.float32).reshape(slot_count)
    d_gating = jnp.sum(jnp.where(seat, home_gating[:, None], 0.0), axis=0)

    me = my_e * n_data + my_d
    my_rows = lax.dynamic_index_in_dim(row_all, me, axis=1, keepdims=False)
    chosen_t = (labels[:, None] == route_ids[None, :]).astype(jnp.float32)
    probs_t = jax.nn.softmax(logits_t + col_last, axis=0)
    gating = experts * jnp.sum(probs_t * chosen_t, axis=0)
    d_logits = (d_gating * gating)[None, :] * (chosen_t - probs_t)
    for k in reversed(range(ITERS)):
        base = logits_t + my_rows[k]
        weighted = chain[k] * jnp.exp(base + col_all[k + 1] - offset)
        pulled = jnp.sum(weighted, axis=0, keepdims=True)
        d_logits = d_logits - weighted + pulled * jnp.exp(base + col_all[k])
    return (d_tokens, d_logits.T, d_gate_weight, d_up_weight, d_down_weight)


def solution(mesh):
    return jax.shard_map(
        body,
        mesh=mesh,
        in_specs=(
            P(("expert", "dp"), None),
            P(("expert", "dp"), None),
            P(("expert", "dp"), None),
            P(("expert", "dp"), None),
            P("expert", "dp", None),
            P("expert", "dp", None),
            P("expert", "dp", None),
        ),
        out_specs=(
            P(("expert", "dp"), None),
            P(("expert", "dp"), None),
            P("expert", "dp", None),
            P("expert", "dp", None),
            P("expert", "dp", None),
        ),
        check_vma=False,
    )
```
